32 devices in a mesh: dp: 8 (over z, x), seq: 4 (over y, core).
Axes of the slice: x: 2, y: 2, z: 4, core: 2. Of those that a mesh axis runs over, the one named last changes fastest.
Arguments:
- hidden_in: bfloat16 [24576, 1024], P(('dp', 'seq')), may hold values from -6 to 6
- key_bias: float32 [8, 3072], P('dp', 'seq'), may hold values from -4 to 4
- w_qkv: bfloat16 [1024, 3072], P('dp'), may hold values from -0.1875 to 0.1875
- bias_q: bfloat16 [1024], P('dp'), may hold values from -3 to 3
- bias_v: bfloat16 [1024], P('dp'), may hold values from -0.75 to 0.75
- w_out: bfloat16 [1024, 1024], P('dp'), may hold values from -3 to 3
- bias_out: bfloat16 [1024], P('dp'), may hold values from -3 to 3
- gain_attn: bfloat16 [1024], P('dp'), may hold values from 0.25 to 1.75
- shift_attn: bfloat16 [1024], P('dp'), may hold values from -3 to 3
- w_up: bfloat16 [1024, 4096], P('dp'), may hold values from -0.1875 to 0.1875
- bias_up: bfloat16 [4096], P('dp'), may hold values from -3 to 3
- w_down: bfloat16 [4096, 1024], P('dp'), may hold values from -0.09375 to 0.09375
- bias_down: bfloat16 [1024], P('dp'), may hold values from -3 to 3
- gain_ffn: bfloat16 [1024], P('dp'), may hold values from 0.25 to 1.75
- shift_ffn: bfloat16 [1024], P('dp'), may hold values from -3 to 3
- grad_out: bfloat16 [24576, 1024], P(('dp', 'seq')), may hold values from -6 to 6
Outputs:
- output: bfloat16 [24576, 1024], P(('dp', 'seq'))
- grad_in: float32 [24576, 1024], P(('dp', 'seq'))
- grad_w_qkv: float32 [1024, 3072], P('dp')
- grad_bias_q: float32 [1024], P('dp')
- grad_bias_v: float32 [1024], P('dp')
- grad_w_out: float32 [1024, 1024], P('dp')
- grad_bias_out: float32 [1024], P('dp')
- grad_gain_attn: float32 [1024], P('dp')
- grad_shift_attn: float32 [1024], P('dp')
- grad_w_up: float32 [1024, 4096], P('dp')
- grad_bias_up: float32 [4096], P('dp')
- grad_w_down: float32 [4096, 1024], P('dp')
- grad_bias_down: float32 [1024], P('dp')
- grad_gain_ffn: float32 [1024], P('dp')
- grad_shift_ffn: float32 [1024], P('dp')
The draws below stay inside these ranges and needn't reach their ends.
All inputs are finite; a program needn't handle non-finite values.
Results may differ from the reference program's by a relative error of at most 0.02.
Values may be sent and summed in bfloat16 or wider, within the bound.
A program may use at most 192 MiB of HBM per device.

```python
import jax
import jax.numpy as jnp
from jax import lax

D = 1024
HEADS = 16
HEAD_DIM = 64
FF = 4096
LENGTH = 3072
SEQS = 8
TOKENS = 24576


def steps_of(rng, dims, shards, low, top_value):
    def one(axis_at, shards_of):
        draws = jax.random.uniform(jax.random.fold_in(jax.random.fold_in(rng, 6), axis_at), (shards_of,), jnp.float32, low / len(shards), top_value / len(shards))
        return jnp.repeat(jnp.exp(draws), dims[axis_at] // shards_of).reshape((-1,) + (1,) * (len(dims) - axis_at - 1))

    loudness = one(*shards[0])
    for cut in shards[1:]:
        loudness = loudness * one(*cut)
    return loudness


def noise(own_key, shape, scale, reach, split=(), kind=jnp.bfloat16):
    array = scale * jax.random.normal(own_key, shape, jnp.float32)
    if split:
        array = array * steps_of(own_key, shape, split, -0.22, 0.18)
    return jnp.clip(array, -reach, reach).astype(kind)


def setup_inputs(seed: int = 0) -> dict:
    keys = jax.random.split(jax.random.key(seed), 17)
    return {
        "hidden_in": noise(keys[0], (TOKENS, D), 1.0, 6.0, ((0, 32),)),
        "key_bias": noise(keys[1], (SEQS, LENGTH), 1.0, 4.0, ((0, 8), (1, 4)), jnp.float32),
        "w_qkv": noise(keys[2], (D, 3 * D), D ** -0.5, 0.1875, ((0, 8),)),
        "bias_q": noise(keys[3], (D,), 0.5, 3.0, ((0, 8),)),
        "bias_v": noise(keys[4], (D,), 0.05, 0.75, ((0, 8),)),
        "w_out": noise(keys[5], (D, D), 4 ** -0.5, 3.0, ((0, 8),)),
        "bias_out": noise(keys[6], (D,), 0.5, 3.0, ((0, 8),)),
        "gain_attn": jnp.clip(1.0 + 0.15 * jax.random.normal(keys[7], (D,), jnp.float32), 0.25, 1.75).astype(jnp.bfloat16),
        "shift_attn": noise(keys[8], (D,), 0.5, 3.0, ((0, 8),)),
        "w_up": noise(keys[9], (D, FF), D ** -0.5, 0.1875, ((0, 8),)),
        "bias_up": noise(keys[10], (FF,), 0.5, 3.0, ((0, 8),)),
        "w_down": noise(keys[11], (FF, D), FF ** -0.5, 0.09375, ((0, 8),)),
        "bias_down": noise(keys[12], (D,), 0.5, 3.0, ((0, 8),)),
        "gain_ffn": jnp.clip(1.0 + 0.15 * jax.random.normal(keys[13], (D,), jnp.float32), 0.25, 1.75).astype(jnp.bfloat16),
        "shift_ffn": noise(keys[14], (D,), 0.5, 3.0, ((0, 8),)),
        "grad_out": noise(keys[15], (TOKENS, D), 1.0, 6.0, ((0, 32),)),
    }


norm_eps = 1e-05

@jax.custom_vjp
def low(v):
    return lax.optimization_barrier(v.astype(jnp.bfloat16)).astype(jnp.float32)

@jax.custom_vjp
def low_back(v):
    return v

def low_keep(v):
    return (low(v), None)

def low_pass(kept, grad):
    return (grad,)

def back_keep(v):
    return (v, None)

def back_low(kept, grad):
    return (low(grad),)
low.defvjp(low_keep, low_pass)
low_back.defvjp(back_keep, back_low)

def matmul(left, right):
    return jnp.dot(left, right, preferred_element_type=jnp.float32, precision=lax.Precision.HIGHEST)

def layer_norm(hidden, gain_vec, shift_vec):
    row_mean = lax.optimization_barrier(jnp.mean(hidden, -1, keepdims=True))
    centered = hidden - row_mean
    row_var = lax.optimization_barrier(jnp.mean(centered * centered, -1, keepdims=True))
    return centered * lax.rsqrt(row_var + norm_eps) * gain_vec + shift_vec

def attend_block(query_blk, keys_all, values_all, bias_row):
    scores = jnp.einsum('bhe,lhe->hbl', query_blk, keys_all, precision=lax.Precision.HIGHEST) * HEAD_DIM ** (-0.5) + bias_row
    scores = low_back(scores)
    row_max = lax.optimization_barrier(jnp.max(scores, -1, keepdims=True))
    expo = jnp.exp(scores - row_max)
    probs = low(expo / lax.optimization_barrier(jnp.sum(expo, -1, keepdims=True)))
    return jnp.einsum('hbl,lhe->bhe', probs, values_all, precision=lax.Precision.HIGHEST)

def attend_sequence(carry_in, item_in):
    heads_all, bias_row = item_in
    block_rows = min(512, LENGTH)
    queries = heads_all[:, 0].reshape(LENGTH // block_rows, block_rows, HEADS, HEAD_DIM)
    keys_all = heads_all[:, 1]
    values_all = heads_all[:, 2]
    blocked = jax.checkpoint(lambda query_blk: attend_block(query_blk, keys_all, values_all, bias_row))
    context = lax.map(blocked, queries)
    return (carry_in, context.reshape(LENGTH, D))

def forward(hidden, key_bias, w_qkv, bias_q, bias_v, w_out, bias_out, gain_attn, shift_attn, w_up, bias_up, w_down, bias_down, gain_ffn, shift_ffn):
    no_bias = jnp.zeros((D,), jnp.float32)
    heads_in = low(low_back(matmul(hidden, w_qkv) + jnp.concatenate([bias_q, no_bias, bias_v])))
    heads_in = heads_in.reshape(SEQS, LENGTH, 3, HEADS, HEAD_DIM)
    _, context = lax.scan(attend_sequence, jnp.zeros((), jnp.float32), (heads_in, key_bias))
    context = low(low_back(context.reshape(TOKENS, D)))
    attended = hidden + low_back(matmul(context, w_out)) + bias_out
    normed = layer_norm(attended, gain_attn, shift_attn)
    pre_act = low_back(matmul(low(normed), w_up)) + bias_up
    activ = low(jax.nn.gelu(pre_act, approximate=False))
    branch_sum = normed + low_back(matmul(activ, w_down)) + bias_down
    return layer_norm(branch_sum, gain_ffn, shift_ffn)

def reference(hidden_in, key_bias, w_qkv, bias_q, bias_v, w_out, bias_out, gain_attn, shift_attn, w_up, bias_up, w_down, bias_down, gain_ffn, shift_ffn, grad_out):
    params = (w_qkv, bias_q, bias_v, w_out, bias_out, gain_attn, shift_attn, w_up, bias_up, w_down, bias_down, gain_ffn, shift_ffn)
    params = tuple((param.astype(jnp.float32) for param in params))
    hidden = hidden_in.astype(jnp.float32)

    def apply_layer(hidden_arg, *param_args):
        return forward(hidden_arg, key_bias, *param_args)
    result, pullback = jax.vjp(apply_layer, hidden, *params)
    grads = pullback(grad_out.astype(jnp.float32))
    return (result.astype(jnp.bfloat16), grads[0], grads[1], grads[2], grads[3], grads[4], grads[5], grads[6], grads[7], grads[8], grads[9], grads[10], grads[11], grads[12], grads[13])
```

```python
import functools

import jax
import jax.numpy as jnp
from jax import lax
from jax.experimental import pallas as pl
from jax.experimental.pallas import tpu as pltpu
from jax.sharding import PartitionSpec as P

HEAD_DIM = 64
LANES = 128
SCALE = HEAD_DIM**-0.5
norm_eps = 1e-05
F32 = jnp.float32
LOW = jnp.bfloat16


def layer_norm(hidden, gain_vec, shift_vec):
    row_mean = jnp.mean(hidden, -1, keepdims=True)
    centered = hidden - row_mean
    row_var = jnp.mean(centered * centered, -1, keepdims=True)
    return centered * lax.rsqrt(row_var + norm_eps) * gain_vec + shift_vec


def gelu_exact(pre_act):
    return jax.nn.gelu(pre_act, approximate=False)


def matmul(left, right):
    return jnp.dot(left, right, preferred_element_type=F32)


def matmul_left(left, right):
    return lax.dot_general(left, right, (((0,), (0,)), ((), ())), preferred_element_type=F32)


def matmul_right(left, right):
    return lax.dot_general(left, right, (((1,), (1,)), ((), ())), preferred_element_type=F32)


def thirds(value):
    first = value.astype(LOW)
    rest = value - first.astype(F32)
    second = rest.astype(LOW)
    third = (rest - second.astype(F32)).astype(LOW)
    return first.astype(F32), second.astype(F32), third.astype(F32)


def head_mask(rows, head):
    lane = lax.broadcasted_iota(jnp.int32, (rows, LANES), 1)
    return (lane < HEAD_DIM) if head == 0 else (lane >= HEAD_DIM)


def fill_keys(k_ref, v_ref, bias_ref, ka_ref, va_ref):
    rows = k_ref.shape[0]
    lane = lax.broadcasted_iota(jnp.int32, (rows, LANES), 1)
    first, second, third = thirds(bias_ref[...])
    extra = jnp.where(
        lane == 0, first, jnp.where(lane == 1, second, jnp.where(lane == 2, third, 1.0))
    )
    ka_ref[:, :LANES] = k_ref[...]
    ka_ref[:, LANES:] = jnp.where(lane < 6, extra, 0.0).astype(LOW)
    va_ref[:, :LANES] = v_ref[...]
    va_ref[:, LANES:] = jnp.where(lane < 3, 1.0, 0.0).astype(LOW)


def forward_kernel(q_ref, k_ref, v_ref, bias_ref, o_ref, qx_ref, ka_ref, va_ref):
    @pl.when(pl.program_id(0) == 0)
    def _():
        fill_keys(k_ref, v_ref, bias_ref, ka_ref, va_ref)

    rows = q_ref.shape[0]
    lane = lax.broadcasted_iota(jnp.int32, (rows, LANES), 1)
    queries = q_ref[...].astype(F32) * SCALE
    ones = jnp.where(lane < 3, 1.0, 0.0)
    outs = []
    for head in range(2):
        masked = jnp.where(head_mask(rows, head), queries, 0.0)
        wide = jnp.concatenate([masked, ones], 1).astype(LOW)
        scores = matmul_right(wide, ka_ref[...])
        row_max = jnp.max(scores, -1, keepdims=True)
        expo = jnp.exp(scores - row_max).astype(LOW)
        both = matmul(expo, va_ref[...])
        total = both[:, LANES : LANES + 1]
        outs.append(both[:, :LANES] / total)
        first, second, third = thirds(row_max + jnp.log(total))
        qx_ref[head] = jnp.where(
            lane == 3, -first, jnp.where(lane == 4, -second, jnp.where(lane == 5, -third, ones))
        ).astype(LOW)
    o_ref[...] = jnp.where(head_mask(rows, 0), outs[0], outs[1]).astype(LOW)


def backward_kernel(
    q_ref, k_ref, v_ref, kt_ref, bias_ref, qx_ref, o_ref, do_ref,
    dq_ref, dk_ref, dv_ref, ka_ref, va_ref, dk_acc, dv_acc, *, chunk,
):
    step = pl.program_id(0)

    @pl.when(step == 0)
    def _():
        fill_keys(k_ref, v_ref, bias_ref, ka_ref, va_ref)
        dk_acc[...] = jnp.zeros_like(dk_acc)
        dv_acc[...] = jnp.zeros_like(dv_acc)

    rows = q_ref.shape[0]
    length = k_ref.shape[0]
    lane = lax.broadcasted_iota(jnp.int32, (rows, LANES), 1)
    queries = q_ref[...].astype(F32) * SCALE
    grads = do_ref[...].astype(F32)
    dots = grads * o_ref[...].astype(F32)
    q_wide, g_wide, q_mask, g_mask = [], [], [], []
    for head in range(2):
        mask = head_mask(rows, head)
        masked = jnp.where(mask, queries, 0.0).astype(LOW)
        g_masked = jnp.where(mask, grads, 0.0).astype(LOW)
        delta = jnp.sum(jnp.where(mask, dots, 0.0), -1, keepdims=True)
        first, second, third = thirds(delta)
        extra = jnp.where(
            lane == 0, -first, jnp.where(lane == 1, -second, jnp.where(lane == 2, -third, 0.0))
        ).astype(LOW)
        q_mask.append(masked)
        g_mask.append(g_masked)
        q_wide.append(jnp.concatenate([masked, qx_ref[head]], 1))
        g_wide.append(jnp.concatenate([g_masked, extra], 1))
    q_rows = jnp.concatenate(q_mask, 0)
    g_rows = jnp.concatenate(g_mask, 0)
    dq_t = [jnp.zeros((LANES, rows), F32) for _ in range(2)]
    for start in range(0, length, chunk):
        part = slice(start, start + chunk)
        p_list, ds_list = [], []
        for head in range(2):
            probs = jnp.exp(matmul_right(ka_ref[part, :], q_wide[head]))
            d_scores = (probs * matmul_right(va_ref[part, :], g_wide[head])).astype(LOW)
            p_list.append(probs.astype(LOW))
            ds_list.append(d_scores)
            dq_t[head] = dq_t[head] + matmul(kt_ref[:, part], d_scores)
        dv_acc[part, :] += matmul(jnp.concatenate(p_list, 1), g_rows)
        dk_acc[part, :] += matmul(jnp.concatenate(ds_list, 1), q_rows)
    row = lax.broadcasted_iota(jnp.int32, (LANES, rows), 0)
    both = jnp.where(row < HEAD_DIM, dq_t[0], dq_t[1]) * SCALE
    dq_ref[...] = both.T.astype(LOW)

    @pl.when(step == pl.num_programs(0) - 1)
    def _():
        dk_ref[...] = dk_acc[...].astype(LOW)
        dv_ref[...] = dv_acc[...].astype(LOW)


def cost(length, matmuls):
    return pl.CostEstimate(
        flops=2 * 2 * matmuls * length * length * 256,
        bytes_accessed=10 * length * LANES * 2,
        transcendentals=2 * length * length,
    )


def attend_forward(queries, keys, values, bias_wide):
    length = queries.shape[0]
    rows = 256
    tile = pl.BlockSpec((rows, LANES), lambda i: (i, 0))
    whole = pl.BlockSpec((length, LANES), lambda i: (0, 0))
    return pl.pallas_call(
        forward_kernel,
        grid=(length // rows,),
        in_specs=[tile, whole, whole, whole],
        out_specs=[tile, pl.BlockSpec((2, rows, LANES), lambda i: (0, i, 0))],
        out_shape=[
            jax.ShapeDtypeStruct((length, LANES), LOW),
            jax.ShapeDtypeStruct((2, length, LANES), LOW),
        ],
        scratch_shapes=[pltpu.VMEM((length, 2 * LANES), LOW)] * 2,
        compiler_params=pltpu.CompilerParams(vmem_limit_bytes=48 * 2**20),
        cost_estimate=cost(length, 2),
    )(queries, keys, values, bias_wide)


def attend_backward(queries, keys, values, bias_wide, q_extra, context, context_grad):
    length = queries.shape[0]
    rows = 256
    chunk = 768 if length % 768 == 0 else 256
    tile = pl.BlockSpec((rows, LANES), lambda i: (i, 0))
    whole = pl.BlockSpec((length, LANES), lambda i: (0, 0))
    return pl.pallas_call(
        functools.partial(backward_kernel, chunk=chunk),
        grid=(length // rows,),
        in_specs=[
            tile, whole, whole, pl.BlockSpec((LANES, length), lambda i: (0, 0)), whole,
            pl.BlockSpec((2, rows, LANES), lambda i: (0, i, 0)), tile, tile,
        ],
        out_specs=[tile, whole, whole],
        out_shape=[jax.ShapeDtypeStruct((length, LANES), LOW)] * 3,
        scratch_shapes=[pltpu.VMEM((length, 2 * LANES), LOW)] * 2
        + [pltpu.VMEM((length, LANES), F32)] * 2,
        compiler_params=pltpu.CompilerParams(vmem_limit_bytes=48 * 2**20),
        cost_estimate=cost(length, 5),
    )(queries, keys, values, keys.T, bias_wide, q_extra, context, context_grad)


def swap(array, name, mask):
    return lax.ppermute(array, name, [(i, i ^ mask) for i in range(lax.axis_size(name))])


def bits(name):
    return lax.axis_size(name).bit_length() - 1


def bit_order(last):
    dp_bits = [("dp", k) for k in reversed(range(bits("dp")))]
    seq_bits = [("seq", k) for k in reversed(range(1, bits("seq")))]
    order = dp_bits + seq_bits
    if last in order:
        order.remove(last)
        order.append(last)
    return order + [("seq", 0)]


def place(name, k):
    return bits("dp") - 1 - k if name == "dp" else bits("dp") + bits("seq") - 1 - k


def my_bit(name, k):
    return (lax.axis_index(name) >> k) & 1


def double(array, name, k):
    other = swap(array, name, 1 << k)
    at = place(name, k)
    return jnp.where(
        my_bit(name, k) == 0,
        jnp.concatenate([array, other], at),
        jnp.concatenate([other, array], at),
    )


def gather_weight(shard, last):
    rows = shard.shape[0] // lax.axis_size("seq")
    own = lax.dynamic_slice_in_dim(shard, lax.axis_index("seq") * rows, rows, 0)
    own = own.reshape((1,) * (bits("dp") + bits("seq")) + own.shape)
    for name, k in bit_order(last):
        own = double(own, name, k)
    return own.reshape(-1, shard.shape[1])


def reduce_weight(grad, last):
    count = bits("dp") + bits("seq")
    rows = grad.shape[0] >> count
    part = grad.astype(LOW).reshape((2,) * count + (rows, grad.shape[1]))
    for name, k in reversed(bit_order(last)):
        mine = my_bit(name, k)
        away = lax.dynamic_index_in_dim(part, 1 - mine, place(name, k))
        keep = lax.dynamic_index_in_dim(part, mine, place(name, k))
        part = (keep.astype(F32) + swap(away, name, 1 << k).astype(F32)).astype(LOW)
    for k in reversed(range(bits("seq"))):
        part = double(part, "seq", k)
    return part.reshape(-1, grad.shape[1]).astype(F32)


def exchange(blocks):
    return [block if t == 0 else swap(block, "seq", t) for t, block in enumerate(blocks)]


def by_index(blocks):
    count = len(blocks)
    me = lax.axis_index("seq")
    return [lax.select_n(me, *[blocks[i ^ j] for i in range(count)]) for j in range(count)]


def columns(array, group, pair, group_width):
    return lax.dynamic_slice_in_dim(array, group * group_width + pair * LANES, LANES, 1)


def local(
    hidden_in, key_bias, w_qkv, bias_q, bias_v, w_out, bias_out, gain_attn, shift_attn,
    w_up, bias_up, w_down, bias_down, gain_ffn, shift_ffn, grad_out,
):
    groups = lax.axis_size("seq")
    me = lax.axis_index("seq")
    tok_rows, width = hidden_in.shape
    group_width = width // groups
    pairs = group_width // LANES
    wide_y, wide_x, wide_z = ("seq", 1), ("dp", 0), ("dp", 1)

    w_q = gather_weight(w_qkv[:, :width], wide_y)
    w_k = gather_weight(w_qkv[:, width : 2 * width], wide_x)
    w_v = gather_weight(w_qkv[:, 2 * width :], wide_z)
    vectors = (
        bias_q, bias_v, bias_out, gain_attn, shift_attn, bias_down, gain_ffn, shift_ffn, bias_up,
    )
    packed = lax.all_gather(jnp.concatenate(vectors), "dp", axis=0).astype(F32)
    fulls, at = [], 0
    for vector in vectors:
        fulls.append(packed[:, at : at + vector.shape[0]].reshape(-1))
        at += vector.shape[0]
    (f_bias_q, f_bias_v, f_bias_out, f_gain_attn, f_shift_attn, f_bias_down, f_gain_ffn,
     f_shift_ffn, f_bias_up) = fulls
    f_w_out = gather_weight(w_out, wide_z)
    f_w_up = gather_weight(w_up, wide_y)
    f_w_down = gather_weight(w_down, wide_x)

    q_rows = (matmul(hidden_in, w_q) + f_bias_q).astype(LOW)
    k_rows = matmul(hidden_in, w_k).astype(LOW)
    v_rows = (matmul(hidden_in, w_v) + f_bias_v).astype(LOW)
    bias_col = jnp.concatenate(exchange([key_bias[0]] * groups))
    bias_wide = jnp.broadcast_to(bias_col[:, None], (bias_col.shape[0], LANES))
    saved, context_parts = [], []
    for pair in range(pairs):
        got = exchange([
            jnp.concatenate(
                [columns(rows, me ^ t, pair, group_width) for rows in (q_rows, k_rows, v_rows)], 1
            )
            for t in range(groups)
        ])
        queries, keys, values = (
            jnp.concatenate([block[:, i * LANES : (i + 1) * LANES] for block in got])
            for i in range(3)
        )
        context, q_extra = attend_forward(queries, keys, values, bias_wide)
        saved.append((queries, keys, values, bias_wide, q_extra, context))
        context_parts.append(by_index(exchange(
            [context[t * tok_rows : (t + 1) * tok_rows] for t in range(groups)]
        )))
    context = jnp.concatenate(
        [context_parts[pair][j] for j in range(groups) for pair in range(pairs)], 1
    )

    attended = hidden_in.astype(F32) + matmul(context, f_w_out) + f_bias_out
    normed = layer_norm(attended, f_gain_attn, f_shift_attn)
    normed_low = normed.astype(LOW)
    pre_act = matmul(normed_low, f_w_up) + f_bias_up
    activ = gelu_exact(pre_act).astype(LOW)
    branch_sum = normed + matmul(activ, f_w_down) + f_bias_down
    output = layer_norm(branch_sum, f_gain_ffn, f_shift_ffn).astype(LOW)

    upstream = grad_out.astype(F32)
    _, norm_back = jax.vjp(layer_norm, branch_sum, f_gain_ffn, f_shift_ffn)
    d_branch, g_gain_ffn, g_shift_ffn = norm_back(upstream)
    g_bias_down = jnp.sum(d_branch, 0)
    d_branch_low = d_branch.astype(LOW)
    g_w_down = matmul_left(activ, d_branch_low).astype(LOW)
    d_activ = matmul_right(d_branch_low, f_w_down)
    _, gelu_back = jax.vjp(gelu_exact, pre_act)
    d_pre = gelu_back(d_activ)[0]
    g_bias_up = jnp.sum(d_pre, 0)
    d_pre_low = d_pre.astype(LOW)
    g_w_up = matmul_left(normed_low, d_pre_low).astype(LOW)
    d_normed = d_branch + matmul_right(d_pre_low, f_w_up)
    _, attn_norm_back = jax.vjp(layer_norm, attended, f_gain_attn, f_shift_attn)
    d_attended, g_gain_attn, g_shift_attn = attn_norm_back(d_normed)
    g_bias_out = jnp.sum(d_attended, 0)
    d_attended_low = d_attended.astype(LOW)
    g_w_out = matmul_left(context, d_attended_low).astype(LOW)
    d_context = matmul_right(d_attended_low, f_w_out).astype(LOW)
    d_context, g_w_down, g_w_up, g_w_out = lax.optimization_barrier(
        (d_context, g_w_down, g_w_up, g_w_out)
    )
    s_w_down = reduce_weight(g_w_down, wide_x)
    s_w_up = reduce_weight(g_w_up, wide_y)
    s_w_out = reduce_weight(g_w_out, wide_z)

    grad_parts = []
    for pair in range(pairs):
        got = jnp.concatenate(exchange(
            [columns(d_context, me ^ t, pair, group_width) for t in range(groups)]
        ))
        d_heads = jnp.concatenate(attend_backward(*saved[pair], got), 1)
        grad_parts.append(by_index(exchange(
            [d_heads[t * tok_rows : (t + 1) * tok_rows] for t in range(groups)]
        )))
    d_q, d_k, d_v = (
        jnp.concatenate(
            [
                grad_parts[pair][j][:, i * LANES : (i + 1) * LANES]
                for j in range(groups)
                for pair in range(pairs)
            ],
            1,
        )
        for i in range(3)
    )
    s_w_q = reduce_weight(matmul_left(hidden_in, d_q), wide_y)
    s_w_k = reduce_weight(matmul_left(hidden_in, d_k), wide_x)
    s_w_v = reduce_weight(matmul_left(hidden_in, d_v), wide_z)
    g_bias_q = jnp.sum(d_q.astype(F32), 0)
    g_bias_v = jnp.sum(d_v.astype(F32), 0)
    grad_in = d_attended + matmul_right(d_q, w_q) + matmul_right(d_k, w_k) + matmul_right(d_v, w_v)

    vector_grads = (
        g_bias_q, g_bias_v, g_bias_out, g_gain_attn, g_shift_attn, g_bias_down, g_gain_ffn,
        g_shift_ffn, g_bias_up,
    )
    shares = lax.axis_size("dp")
    rows = jnp.concatenate([g.reshape(shares, -1) for g in vector_grads], 1).astype(LOW)
    own = lax.dynamic_index_in_dim(
        lax.psum(rows, ("dp", "seq")), lax.axis_index("dp"), 0, False
    ).astype(F32)
    sums, at = [], 0
    for vector in vectors:
        sums.append(own[at : at + vector.shape[0]])
        at += vector.shape[0]
    (s_bias_q, s_bias_v, s_bias_out, s_gain_attn, s_shift_attn, s_bias_down, s_gain_ffn,
     s_shift_ffn, s_bias_up) = sums
    return (
        output, grad_in, jnp.concatenate([s_w_q, s_w_k, s_w_v], 1), s_bias_q, s_bias_v, s_w_out,
        s_bias_out, s_gain_attn, s_shift_attn, s_w_up, s_bias_up, s_w_down, s_bias_down,
        s_gain_ffn, s_shift_ffn,
    )


def solution(mesh):
    tokens = P(("dp", "seq"), None)
    matrix = P("dp", None)
    vector = P("dp")
    return jax.shard_map(
        local,
        mesh=mesh,
        in_specs=(
            tokens, P("dp", "seq"), matrix, vector, vector, matrix, vector, vector, vector,
            matrix, vector, matrix, vector, vector, vector, tokens,
        ),
        out_specs=(
            tokens, tokens, matrix, vector, vector, matrix, vector, vector, vector, matrix,
            vector, matrix, vector, vector, vector,
        ),
        check_vma=False,
    )
```
